1024 devices in a mesh: dp: 32 (over y_lo, x), fsdp: 32 (over y_hi, z, core).
Axes of the slice: x: 8, y: 8 (y_hi: 2, y_lo: 4; y = y_hi * 4 + y_lo), z: 8, core: 2. Of those that a mesh axis runs over, the one named last changes fastest.
Arguments:
- q_raw: bfloat16 [32, 32, 128, 1664], P('dp', 'fsdp'), may hold values from -6 to 6
- k_raw: bfloat16 [32, 32, 128, 1664], P('dp', 'fsdp'), may hold values from -6 to 6
- v_raw: bfloat16 [32, 32, 128, 1664], P('dp', 'fsdp'), may hold values from -6 to 6
- gain_q: float32 [1664], P('fsdp'), may hold values from 0.1 to 1.9
- gain_k: float32 [1664], P('fsdp'), may hold values from 0.1 to 1.9
- dest: int32 [32, 32, 128], P('dp', 'fsdp'), may hold values from 0 to 31, as said below
- slot: int32 [32, 32, 128], P('dp', 'fsdp'), may hold values from 0 to 4, as said below
- recv_image: int32 [32, 32, 160], P('dp', 'fsdp'), may hold values from -1 to 1, as said below
- d_attended: bfloat16 [32, 32, 160, 1664], P('dp', 'fsdp'), may hold values from -6 to 6
Outputs:
- attended: bfloat16 [32, 32, 160, 1664], P('dp', 'fsdp')
- grad_q: bfloat16 [32, 32, 128, 1664], P('dp', 'fsdp')
- grad_k: bfloat16 [32, 32, 128, 1664], P('dp', 'fsdp')
- grad_v: bfloat16 [32, 32, 128, 1664], P('dp', 'fsdp')
- grad_gain_q: float32 [1664], P('fsdp')
- grad_gain_k: float32 [1664], P('fsdp')
The draws below stay inside these ranges and needn't reach their ends.
Inputs may be any that keep to these rules, and one draw needn't show every extreme that they name: `dest`: from one device at most 5 tokens go to one destination, and in every device all 5 slots of some destination are used. No two tokens of one device share both dest and slot. `recv_image`: A received slot i * 5 + c holds -1 exactly when no token of device i is sent to that slot, else the image number of its token; all tokens that one device sends to one destination belong to one image.
All inputs are finite; a program needn't handle non-finite values.
Results may differ from the reference program's by a relative error of at most 0.0085.
Values may be sent and summed in bfloat16 or wider, within the bound.
A program may use at most 64 MiB of HBM per device.

```python
import jax
import jax.numpy as jnp
from jax import lax

HDIM = 128
D = 1664
TOK = 128
IMAGES = 2
C = 5
R = 160
N_DP = 32
N_FSDP = 32


def routing(key):
    slot_total = N_DP * C
    unit_count = N_DP * N_FSDP
    unit_keys = jax.random.split(jax.random.fold_in(key, 101), unit_count)

    def per_device(device_key):
        first_key, second_key, third_key = jax.random.split(device_key, 3)
        ranking = jax.random.permutation(first_key, slot_total)
        chosen_dest = jax.random.randint(second_key, (), 0, N_DP)
        owners = jnp.arange(slot_total) // C
        priority = jnp.where(owners == chosen_dest, 0, slot_total) + ranking
        ordering = jnp.argsort(priority, stable=True)
        chosen_slots = ordering[:TOK]
        return jax.random.permutation(third_key, chosen_slots)
    assigned = jax.vmap(per_device)(unit_keys).reshape(N_DP, N_FSDP, TOK).astype(jnp.int32)
    return ((assigned // C).astype(jnp.int32), (assigned % C).astype(jnp.int32))


def draw_q_raw(key, part):
    key = jax.random.fold_in(key, 11)
    array_shape = (N_DP, N_FSDP, TOK, D)
    result = jax.random.normal(key, array_shape, jnp.float32)
    return jnp.clip(result, -6.0, 6.0).astype(jnp.bfloat16)


def draw_k_raw(key, part):
    key = jax.random.fold_in(key, 12)
    array_shape = (N_DP, N_FSDP, TOK, D)
    result = jax.random.normal(key, array_shape, jnp.float32)
    return jnp.clip(result, -6.0, 6.0).astype(jnp.bfloat16)


def draw_dest(key, part):
    dest_index, slot_index = routing(key)
    return dest_index


def draw_slot(key, part):
    dest_index, slot_index = routing(key)
    return slot_index


def draw_recv_image(key, part):
    dest_index, slot_index = routing(key)
    key = jax.random.fold_in(key, 7)
    source_rank = jnp.arange(N_DP, dtype=jnp.int32)[:, None, None]
    fsdp_rank = jnp.arange(N_FSDP, dtype=jnp.int32)[None, :, None]
    filled = jnp.zeros((N_DP, N_FSDP, N_DP, C), jnp.int32)
    filled = filled.at[dest_index, fsdp_rank, source_rank, slot_index].set(1)
    block_images = jax.random.randint(key, (N_DP, N_FSDP, N_DP, 1), 0, IMAGES)
    image_ids = jnp.broadcast_to(block_images, (N_DP, N_FSDP, N_DP, C))
    return jnp.where(filled > 0, image_ids, -1).reshape(N_DP, N_FSDP, N_DP * C).astype(jnp.int32)


def steps_of(key, extent, cuts, low, top_value):
    factor_of = 1.0
    for dim, shards_of in cuts:
        heights = jax.random.uniform(jax.random.fold_in(jax.random.fold_in(key, 6), dim), (shards_of,), jnp.float32, low / len(cuts), top_value / len(cuts))
        factor_of = factor_of * jnp.repeat(jnp.exp(heights), extent[dim] // shards_of).reshape((-1,) + (1,) * (len(extent) - 1 - dim))
    return factor_of


def normal_values(key, shape, deviation, reach, pieces=(), kind=jnp.bfloat16):
    loudness = steps_of(key, shape, pieces, -0.22, 0.18) if pieces else 1.0
    array = jax.random.normal(key, shape, jnp.float32) * deviation * loudness
    return jnp.minimum(jnp.maximum(array, -reach), reach).astype(kind)


def setup_inputs(seed: int = 0) -> dict:
    splits = jax.random.split(jax.random.key(seed), 10)
    return {
        "q_raw": draw_q_raw(jax.random.fold_in(splits[9], 71), 0),
        "k_raw": draw_k_raw(jax.random.fold_in(splits[9], 71), 0),
        "v_raw": normal_values(splits[2], (N_DP, N_FSDP, TOK, D), 1.0, 6.0, ((0, 32), (1, 32))),
        "gain_q": jnp.clip(1.0 + 0.18 * jax.random.normal(splits[3], (D,), jnp.float32), 0.1, 1.9),
        "gain_k": jnp.clip(1.0 + 0.18 * jax.random.normal(splits[4], (D,), jnp.float32), 0.1, 1.9),
        "dest": draw_dest(jax.random.fold_in(splits[9], 71), 0),
        "slot": draw_slot(jax.random.fold_in(splits[9], 71), 0),
        "recv_image": draw_recv_image(jax.random.fold_in(splits[9], 71), 0),
        "d_attended": normal_values(splits[8], (N_DP, N_FSDP, R, D), 1.0, 6.0, ((0, 32), (1, 32))),
    }


def normalize_rows(raw_rows, gain_full):
    as_float = raw_rows.astype(jnp.float32)
    inverse = lax.rsqrt(lax.optimization_barrier(jnp.mean(as_float * as_float, axis=-1, keepdims=True)) + 1e-06)
    unit_rows = as_float * inverse
    return ((unit_rows * gain_full).astype(jnp.bfloat16), unit_rows, inverse)

def restore_rows(grad_norm, unit_rows, inverse, gain_full):
    partial_sum = lax.optimization_barrier(jnp.sum(grad_norm * unit_rows, axis=0))
    grad_unit = grad_norm * gain_full
    grad_raw = inverse * (grad_unit - unit_rows * lax.optimization_barrier(jnp.mean(grad_unit * unit_rows, axis=-1, keepdims=True)))
    return (grad_raw, partial_sum)

def attend_block(query_norm, key_norm, value_rows, segments, grad_out):
    slot_count, feature_width = query_norm.shape
    head_count = feature_width // HDIM
    scaling = 1.0 / HDIM ** 0.5
    query_heads = query_norm.reshape(slot_count, head_count, HDIM).astype(jnp.float32)
    key_heads = key_norm.reshape(slot_count, head_count, HDIM).astype(jnp.float32)
    value_heads = value_rows.reshape(slot_count, head_count, HDIM).astype(jnp.float32)
    grad_heads = grad_out.reshape(slot_count, head_count, HDIM).astype(jnp.float32)
    allowed = (segments[:, None] == segments[None, :]) & (segments[None, :] >= 0)
    scores = jnp.einsum('qhd,khd->hqk', query_heads, key_heads) * scaling
    scores = jnp.where(allowed[None], scores, -1e+30)
    highest = lax.optimization_barrier(jnp.max(scores, axis=-1, keepdims=True))
    weights = jnp.where(allowed[None], jnp.exp(scores - highest), 0.0)
    denominator = lax.optimization_barrier(jnp.sum(weights, axis=-1, keepdims=True))
    denominator = jnp.where(denominator > 0, denominator, 1.0)
    probs = weights / denominator
    probs_low = probs.astype(jnp.bfloat16)
    probs_wide = probs_low.astype(jnp.float32)
    attended = jnp.einsum('hqk,khd->qhd', probs_wide, value_heads).reshape(slot_count, feature_width).astype(jnp.bfloat16)
    grad_probs = jnp.einsum('qhd,khd->hqk', grad_heads, value_heads)
    grad_values = jnp.einsum('hqk,qhd->khd', probs_wide, grad_heads).reshape(slot_count, feature_width).astype(jnp.bfloat16)
    inner = lax.optimization_barrier(jnp.sum(grad_probs * probs, axis=-1, keepdims=True))
    grad_scores = (probs * (grad_probs - inner) * scaling).astype(jnp.bfloat16).astype(jnp.float32)
    grad_query = jnp.einsum('hqk,khd->qhd', grad_scores, key_heads).reshape(slot_count, feature_width)
    grad_key = jnp.einsum('hqk,qhd->khd', grad_scores, query_heads).reshape(slot_count, feature_width)
    return (attended, grad_query, grad_key, grad_values)

def reference(q_raw, k_raw, v_raw, gain_q, gain_k, dest, slot, recv_image, d_attended):
    dp_count, fsdp_count, tokens, feature_width = q_raw.shape
    capacity = C
    received = dp_count * capacity
    source_rank = jnp.arange(dp_count, dtype=jnp.int32)[:, None, None]
    fsdp_rank = jnp.arange(fsdp_count, dtype=jnp.int32)[None, :, None]

    def spread(values_in):
        buffer = jnp.zeros((dp_count, fsdp_count, dp_count, capacity, feature_width), values_in.dtype)
        buffer = buffer.at[dest, fsdp_rank, source_rank, slot].set(values_in)
        return buffer.reshape(dp_count * fsdp_count, received, feature_width)

    def per_receiver(operands):
        query_in, key_in, value_in, segments, grad_out = operands
        query_norm, unit_q, inverse_q = normalize_rows(query_in, gain_q)
        key_norm, unit_k, inverse_k = normalize_rows(key_in, gain_k)
        attended, grad_qn, grad_kn, grad_values = attend_block(query_norm, key_norm, value_in, segments, grad_out)
        grad_qr, part_q = restore_rows(grad_qn, unit_q, inverse_q, gain_q)
        grad_kr, part_k = restore_rows(grad_kn, unit_k, inverse_k, gain_k)
        return (attended, grad_qr.astype(jnp.bfloat16), grad_kr.astype(jnp.bfloat16), grad_values, part_q, part_k)
    results = lax.map(per_receiver, (spread(q_raw), spread(k_raw), spread(v_raw), recv_image.reshape(dp_count * fsdp_count, received), d_attended.reshape(dp_count * fsdp_count, received, feature_width)))
    attended = results[0].reshape(dp_count, fsdp_count, received, feature_width)

    def gather_home(balanced):
        shaped = balanced.reshape(dp_count, fsdp_count, dp_count, capacity, feature_width)
        return shaped[dest, fsdp_rank, source_rank, slot]
    grad_gain_q = lax.optimization_barrier(jnp.sum(results[4], axis=0))
    grad_gain_k = lax.optimization_barrier(jnp.sum(results[5], axis=0))
    return (attended, gather_home(results[1]), gather_home(results[2]), gather_home(results[3]), grad_gain_q, grad_gain_k)
```

```python
import functools

import jax
import jax.numpy as jnp
from jax import lax
from jax.experimental import pallas as pl
from jax.experimental.pallas import tpu as pltpu
from jax.sharding import PartitionSpec as P

HDIM = 128
TILE = 16
PER = 3
EPS = 1e-06
MASKED = -1e30
F32 = jnp.float32
BF16 = jnp.bfloat16
MESH = pl.DeviceIdType.MESH


def dot(a, b, dims=((1,), (0,))):
    return lax.dot_general(a, b, (dims, ((), ())), preferred_element_type=F32)


def iota(shape, dim):
    return lax.broadcasted_iota(jnp.int32, shape, dim)


def as_column(row):
    n = row.shape[1]
    same = iota((n, n), 0) == iota((n, n), 1)
    return jnp.sum(jnp.where(same, row, 0), axis=1, keepdims=True)


def head_lanes(head):
    start = head * HDIM
    if not isinstance(head, int):
        start = pl.multiple_of(start, HDIM)
    return pl.ds(start, HDIM)


def kernel(
    n_dp, n_fsdp, cap, heads, piece,
    q_hbm, k_hbm, v_hbm, do_hbm, gq_ref, gk_ref, dest_ref, slot_ref, seg_ref,
    att_ref, grad_q_ref, grad_k_ref, grad_v_ref, ggq_ref, ggk_ref,
    q_in, k_in, v_in, do_in,
    pick, unpick, pack_r, unpack_r, bias, inv_q, inv_k,
    fwd_send, fwd_recv, ret_send, ret_recv,
    gtmp, gsend, grecv, gain_q, gain_k,
    part, rs_recv, ar_send, ar_recv,
    dqn, dkn, acc_q, acc_k,
    load_sem, fs_sem, fr_sem, bs_sem, br_sem, gs_sem, gr_sem,
):
    tokens = q_in.shape[0]
    width = q_in.shape[1]
    slots = n_dp * cap
    full = heads // PER
    left = heads % PER
    halves = n_dp // TILE
    hrow = TILE * cap
    scaling = 1.0 / HDIM**0.5
    me_d = lax.axis_index("dp")
    me_f = lax.axis_index("fsdp")

    loads = [
        pltpu.make_async_copy(src, dst, load_sem.at[i])
        for i, (src, dst) in enumerate(
            ((v_hbm, v_in), (q_hbm, q_in), (k_hbm, k_in), (do_hbm, do_in))
        )
    ]
    for load in loads:
        load.start()

    barrier = pltpu.get_barrier_semaphore()

    def greet_dp(s, carry):
        pl.semaphore_signal(
            barrier, inc=1, device_id={"dp": lax.rem(me_d + s, n_dp)}, device_id_type=MESH
        )
        return carry

    def greet_fsdp(s, carry):
        pl.semaphore_signal(
            barrier, inc=1, device_id={"fsdp": lax.rem(me_f + s, n_fsdp)}, device_id_type=MESH
        )
        return carry

    lax.fori_loop(1, n_fsdp, greet_fsdp, 0)
    lax.fori_loop(1, n_dp, greet_dp, 0)

    offset = me_f * piece
    lane0 = lax.rem(offset, HDIM)
    gtmp[...] = jnp.zeros_like(gtmp)
    gtmp[0:1, 0:piece] = gq_ref[...]
    gtmp[1:2, 0:piece] = gk_ref[...]
    placed = pltpu.roll(gtmp[...], lane0, 1)
    gsend[...] = jnp.zeros_like(gsend)
    gsend[0:2, :] = placed[0:2, :HDIM]
    gsend[4:6, :] = placed[0:2, HDIM:]
    grecv[me_f] = gsend[...]

    route = dest_ref[...] * TILE + slot_ref[...]
    rows = iota((n_dp * TILE, tokens), 0)
    route_col = as_column(route)
    cols = iota((tokens, n_dp * TILE), 1)
    for j in range(PER):
        lanes = slice(j * tokens, (j + 1) * tokens)
        pick[:, lanes] = jnp.where(rows == route + j * cap, 1.0, 0.0).astype(BF16)
        unpick[lanes, :] = jnp.where(cols == route_col + j * cap, 1.0, 0.0).astype(BF16)

    def send_tiles(src, dst, first, count, send_sem, recv_sem):
        def one(s, carry):
            peer = lax.rem(me_d + s, n_dp)
            pltpu.make_async_remote_copy(
                src_ref=src.at[peer, pl.ds(first, count)],
                dst_ref=dst.at[me_d, pl.ds(first, count)],
                send_sem=send_sem,
                recv_sem=recv_sem,
                device_id={"dp": peer},
                device_id_type=MESH,
            ).start()
            return carry

        lax.fori_loop(1, n_dp, one, 0)
        dst[me_d, pl.ds(first, count)] = src[me_d, pl.ds(first, count)]

    def wait_tiles(buf, first, count, sem):
        ref = buf.at[pl.ds(0, n_dp - 1), pl.ds(first, count)]
        pltpu.make_async_copy(ref, ref, sem).wait()

    def pack(blocks, tile):
        out = dot(pick[...], jnp.concatenate(blocks, axis=0)).astype(BF16)
        fwd_send[:, tile] = out.reshape(n_dp, TILE, HDIM)

    loads[0].wait()

    def pack_v(t, carry):
        pack([v_in[:, head_lanes(t * PER + j)] for j in range(PER)], t)
        return carry

    lax.fori_loop(0, full, pack_v, 0)

    pl.semaphore_wait(barrier, n_dp + n_fsdp - 2)

    def send_gain(s, carry):
        peer = lax.rem(me_f + s, n_fsdp)
        pltpu.make_async_remote_copy(
            src_ref=gsend,
            dst_ref=grecv.at[me_f],
            send_sem=gs_sem.at[0],
            recv_sem=gr_sem.at[0],
            device_id={"fsdp": peer},
            device_id_type=MESH,
        ).start()
        return carry

    def wait_small(buf, sem, n):
        ref = buf.at[pl.ds(0, n - 1)]
        pltpu.make_async_copy(ref, ref, sem).wait()

    lax.fori_loop(1, n_fsdp, send_gain, 0)
    send_tiles(fwd_send, fwd_recv, 0, full, fs_sem.at[full], fr_sem.at[full])

    big = iota((PER * hrow, TILE * TILE), 0)
    small = iota((PER * hrow, TILE * TILE), 1)
    block, inner_row = big // hrow, big % hrow
    want = (inner_row // cap) * TILE + block * cap + inner_row % cap
    unpack_r[...] = jnp.where(want == small, 1.0, 0.0).astype(BF16)
    small = iota((TILE * TILE, PER * hrow), 0)
    big = iota((TILE * TILE, PER * hrow), 1)
    block, inner_row = big // hrow, big % hrow
    want = (inner_row // cap) * TILE + block * cap + inner_row % cap
    pack_r[...] = jnp.where(want == small, 1.0, 0.0).astype(BF16)
    seg_row = seg_ref[...]
    seg_col = as_column(seg_row)
    bias[...] = jnp.where((seg_col == seg_row) & (seg_col >= 0), 0.0, MASKED)

    def inverse(src, dst):
        total = jnp.zeros((tokens, HDIM), F32)
        for h in range(heads):
            x = src[:, head_lanes(h)].astype(F32)
            total = total + x * x
        mean = jnp.sum(total, axis=1, keepdims=True) * (1.0 / width)
        dst[...] = jnp.broadcast_to(lax.rsqrt(mean + EPS), (tokens, HDIM))

    loads[1].wait()
    inverse(q_in, inv_q)
    loads[2].wait()
    inverse(k_in, inv_k)

    wait_small(grecv, gr_sem.at[0], n_fsdp)
    for h in range(heads):
        for which, dst in ((0, gain_q), (1, gain_k)):
            total = jnp.zeros((1, HDIM), F32)
            for i in range(n_fsdp):
                first = i * piece // HDIM
                last = (i * piece + piece - 1) // HDIM
                if first == h:
                    total = total + grecv[i, which : which + 1, :]
                elif last == h:
                    total = total + grecv[i, which + 4 : which + 5, :]
            dst[h : h + 1, :] = total

    def norm_block(src, inv, gain, h):
        x = src[:, head_lanes(h)].astype(F32)
        return (x * inv[...] * gain[pl.ds(h, 1), :]).astype(BF16)

    def q_block(h):
        return norm_block(q_in, inv_q, gain_q, h)

    def k_block(h):
        return norm_block(k_in, inv_k, gain_k, h)

    def pack_qk(g, carry):
        h = g * PER
        t = full + 2 * g
        pack([q_block(h), k_block(h), q_block(h + 1)], t)
        pack([k_block(h + 1), q_block(h + 2), k_block(h + 2)], t + 1)
        send_tiles(fwd_send, fwd_recv, t, 2, fs_sem.at[g], fr_sem.at[g])
        return carry

    lax.fori_loop(0, full, pack_qk, 0)
    for i in range(left):
        h = full * PER + i
        pack([q_block(h), k_block(h), v_in[:, head_lanes(h)]], 3 * full + i)
    if left:
        send_tiles(
            fwd_send, fwd_recv, 3 * full, left, fs_sem.at[full + 1], fr_sem.at[full + 1]
        )

    def unpack(buf, tile):
        out = []
        for a in range(halves):
            x = buf[a * TILE : (a + 1) * TILE, tile].reshape(TILE * TILE, HDIM)
            out.append(dot(unpack_r[...], x).astype(BF16))
        return [
            jnp.concatenate([o[j * hrow : (j + 1) * hrow] for o in out], axis=0)
            for j in range(PER)
        ]

    def pack_back(blocks, tile):
        for a in range(halves):
            x = jnp.concatenate([b[a * hrow : (a + 1) * hrow] for b in blocks], axis=0)
            out = dot(pack_r[...], x).astype(BF16)
            ret_send[a * TILE : (a + 1) * TILE, tile] = out.reshape(TILE, TILE, HDIM)

    valid = jnp.where(seg_row >= 0, 1.0, 0.0)

    def attend(h, q, k, v):
        do = do_in[:, head_lanes(h)]
        st = dot(k, q, ((1,), (1,))) * scaling + bias[...]
        w = jnp.exp(st - jnp.max(st, axis=0, keepdims=True))
        pt = w * (valid / jnp.sum(w, axis=0, keepdims=True))
        ptb = pt.astype(BF16)
        att_ref[:, head_lanes(h)] = dot(ptb, v, ((0,), (0,))).astype(BF16)
        dpt = dot(v, do, ((1,), (1,)))
        inner = jnp.sum(dpt * pt, axis=0, keepdims=True)
        dst = (pt * (dpt - inner) * scaling).astype(BF16)
        dv = dot(ptb, do).astype(BF16)
        dk = dot(dst, q)
        dq = dot(dst, k, ((0,), (0,)))
        sum_q = jnp.sum(dq * q.astype(F32), axis=0, keepdims=True)
        sum_k = jnp.sum(dk * k.astype(F32), axis=0, keepdims=True)
        part[h + 1, 0:1, :] = sum_q
        part[h + 1, 1:2, :] = sum_k
        part[h, 4:5, :] = sum_q
        part[h, 5:6, :] = sum_k
        return dq.astype(BF16), dk.astype(BF16), dv

    part[...] = jnp.zeros_like(part)
    loads[3].wait()
    wait_tiles(fwd_recv, 0, full, fr_sem.at[full])

    def group(g, carry):
        h = g * PER
        t = full + 2 * g
        wait_tiles(fwd_recv, t, 2, fr_sem.at[g])
        v0, v1, v2 = unpack(fwd_recv, g)
        q0, k0, q1 = unpack(fwd_recv, t)
        k1, q2, k2 = unpack(fwd_recv, t + 1)
        dq0, dk0, dv0 = attend(h, q0, k0, v0)
        dq1, dk1, dv1 = attend(h + 1, q1, k1, v1)
        dq2, dk2, dv2 = attend(h + 2, q2, k2, v2)
        pack_back([dq0, dk0, dq1], 3 * g)
        pack_back([dk1, dq2, dk2], 3 * g + 1)
        pack_back([dv0, dv1, dv2], 3 * g + 2)
        send_tiles(ret_send, ret_recv, 3 * g, 3, bs_sem.at[g], br_sem.at[g])
        return carry

    lax.fori_loop(0, full, group, 0)
    if left:
        wait_tiles(fwd_recv, 3 * full, left, fr_sem.at[full + 1])
        for i in range(left):
            h = full * PER + i
            q, k, v = unpack(fwd_recv, 3 * full + i)
            pack_back(attend(h, q, k, v), 3 * full + i)
        send_tiles(ret_send, ret_recv, 3 * full, left, bs_sem.at[full], br_sem.at[full])

    def scatter(s, carry):
        peer = lax.rem(me_f + s, n_fsdp)
        pltpu.make_async_remote_copy(
            src_ref=part.at[(peer * piece) // HDIM + 1],
            dst_ref=rs_recv.at[me_f],
            send_sem=gs_sem.at[1],
            recv_sem=gr_sem.at[1],
            device_id={"fsdp": peer},
            device_id_type=MESH,
        ).start()
        return carry

    lax.fori_loop(1, n_fsdp, scatter, 0)
    rs_recv[me_f] = part[offset // HDIM + 1]

    def unpack_home(tile):
        x = ret_recv[:, tile].reshape(n_dp * TILE, HDIM)
        out = dot(unpick[...], x)
        return [out[j * tokens : (j + 1) * tokens] for j in range(PER)]

    def keep(h, grad, raw, inv, gain, dst, acc):
        unit = raw[:, head_lanes(h)].astype(F32) * inv[...]
        acc[...] += grad * gain[pl.ds(h, 1), :] * unit
        dst[:, head_lanes(h)] = grad.astype(BF16)

    def keep_q(h, grad):
        keep(h, grad, q_in, inv_q, gain_q, dqn, acc_q)

    def keep_k(h, grad):
        keep(h, grad, k_in, inv_k, gain_k, dkn, acc_k)

    acc_q[...] = jnp.zeros_like(acc_q)
    acc_k[...] = jnp.zeros_like(acc_k)

    def home(g):
        h = g * PER
        wait_tiles(ret_recv, 3 * g, 3, br_sem.at[g])
        dq0, dk0, dq1 = unpack_home(3 * g)
        keep_q(h, dq0)
        keep_k(h, dk0)
        keep_q(h + 1, dq1)
        dk1, dq2, dk2 = unpack_home(3 * g + 1)
        keep_k(h + 1, dk1)
        keep_q(h + 2, dq2)
        keep_k(h + 2, dk2)
        for j, dv in enumerate(unpack_home(3 * g + 2)):
            grad_v_ref[:, head_lanes(h + j)] = dv.astype(BF16)

    def home_step(g, carry):
        home(g)
        return carry

    early = full - 1
    lax.fori_loop(0, early, home_step, 0)

    wait_small(rs_recv, gr_sem.at[1], n_fsdp)
    ar_send[...] = jnp.sum(rs_recv[...], axis=0)

    def share(s, carry):
        pltpu.make_async_remote_copy(
            src_ref=ar_send,
            dst_ref=ar_recv.at[me_d],
            send_sem=gs_sem.at[2],
            recv_sem=gr_sem.at[2],
            device_id={"dp": lax.rem(me_d + s, n_dp)},
            device_id_type=MESH,
        ).start()
        return carry

    lax.fori_loop(1, n_dp, share, 0)
    ar_recv[me_d] = ar_send[...]

    lax.fori_loop(early, full, home_step, 0)

    wait_small(ar_recv, gr_sem.at[2], n_dp)
    total = jnp.sum(ar_recv[...], axis=0)
    gtmp[:, :HDIM] = total
    gtmp[0:2, HDIM:] = total[4:6, :]
    mine = pltpu.roll(gtmp[...], lax.rem(2 * HDIM - lane0, 2 * HDIM), 1)
    ggq_ref[...] = mine[0:1, 0:piece] / gq_ref[...]
    ggk_ref[...] = mine[1:2, 0:piece] / gk_ref[...]

    if left:
        wait_tiles(ret_recv, 3 * full, left, br_sem.at[full])
        for i in range(left):
            h = full * PER + i
            dq, dk, dv = unpack_home(3 * full + i)
            keep_q(h, dq)
            keep_k(h, dk)
            grad_v_ref[:, head_lanes(h)] = dv.astype(BF16)

    for raw, inv, gain, src, acc, dst in (
        (q_in, inv_q, gain_q, dqn, acc_q, grad_q_ref),
        (k_in, inv_k, gain_k, dkn, acc_k, grad_k_ref),
    ):
        mean = jnp.sum(acc[...], axis=1, keepdims=True) * (1.0 / width)
        factor = inv[...]
        for h in range(heads):
            lanes = head_lanes(h)
            unit = raw[:, lanes].astype(F32) * factor
            grad = src[:, lanes].astype(F32) * gain[h : h + 1, :]
            dst[:, lanes] = (factor * (grad - unit * mean)).astype(BF16)

    for g in range(full):
        wait_tiles(fwd_send, full + 2 * g, 2, fs_sem.at[g])
        wait_tiles(ret_send, 3 * g, 3, bs_sem.at[g])
    wait_tiles(fwd_send, 0, full, fs_sem.at[full])
    if left:
        wait_tiles(fwd_send, 3 * full, left, fs_sem.at[full + 1])
        wait_tiles(ret_send, 3 * full, left, bs_sem.at[full])
    wait_small(grecv, gs_sem.at[0], n_fsdp)
    wait_small(rs_recv, gs_sem.at[1], n_fsdp)
    wait_small(ar_recv, gs_sem.at[2], n_dp)


def shards(q_raw, k_raw, v_raw, gain_q, gain_k, dest, slot, recv_image, d_attended):
    tokens, width = q_raw.shape[2:]
    n_dp, n_fsdp = lax.axis_size("dp"), lax.axis_size("fsdp")
    slots = recv_image.shape[2]
    cap = slots // n_dp
    heads = width // HDIM
    piece = gain_q.shape[0]
    full, left = heads // PER, heads % PER
    tiles = 3 * full + left
    vmem = pl.BlockSpec(memory_space=pltpu.VMEM)
    hbm = pl.BlockSpec(memory_space=pl.ANY)
    rows = pltpu.VMEM((tokens, width), BF16)
    moved = pltpu.VMEM((n_dp, tiles, TILE, HDIM), BF16)
    square = pltpu.VMEM((tokens, HDIM), F32)
    sem = pltpu.SemaphoreType.DMA
    hrow = TILE * cap
    grid_rows = (heads + 15) // 8 * 8
    outs = pl.pallas_call(
        functools.partial(kernel, n_dp, n_fsdp, cap, heads, piece),
        out_shape=(
            jax.ShapeDtypeStruct((slots, width), BF16),
            jax.ShapeDtypeStruct((tokens, width), BF16),
            jax.ShapeDtypeStruct((tokens, width), BF16),
            jax.ShapeDtypeStruct((tokens, width), BF16),
            jax.ShapeDtypeStruct((1, piece), F32),
            jax.ShapeDtypeStruct((1, piece), F32),
        ),
        in_specs=[hbm] * 4 + [vmem] * 5,
        out_specs=[vmem] * 6,
        scratch_shapes=[
            rows, rows, rows, pltpu.VMEM((slots, width), BF16),
            pltpu.VMEM((n_dp * TILE, PER * tokens), BF16),
            pltpu.VMEM((PER * tokens, n_dp * TILE), BF16),
            pltpu.VMEM((TILE * TILE, PER * hrow), BF16),
            pltpu.VMEM((PER * hrow, TILE * TILE), BF16),
            pltpu.VMEM((slots, slots), F32),
            square, square,
            moved, moved, moved, moved,
            pltpu.VMEM((8, 2 * HDIM), F32),
            pltpu.VMEM((8, HDIM), F32),
            pltpu.VMEM((n_fsdp, 8, HDIM), F32),
            pltpu.VMEM((grid_rows, HDIM), F32),
            pltpu.VMEM((grid_rows, HDIM), F32),
            pltpu.VMEM((heads + 1, 8, HDIM), F32),
            pltpu.VMEM((n_fsdp, 8, HDIM), F32),
            pltpu.VMEM((8, HDIM), F32),
            pltpu.VMEM((n_dp, 8, HDIM), F32),
            rows, rows, square, square,
            sem((4,)), sem((full + 2,)), sem((full + 2,)), sem((full + 1,)), sem((full + 1,)),
            sem((3,)), sem((3,)),
        ],
        compiler_params=pltpu.CompilerParams(
            collective_id=0, has_side_effects=True, vmem_limit_bytes=48 * 1024 * 1024
        ),
        name="route_attend",
    )(
        q_raw.reshape(tokens, width),
        k_raw.reshape(tokens, width),
        v_raw.reshape(tokens, width),
        d_attended.reshape(slots, width),
        gain_q.reshape(1, piece),
        gain_k.reshape(1, piece),
        dest.reshape(1, tokens),
        slot.reshape(1, tokens),
        recv_image.reshape(1, slots),
    )
    attended, grad_q, grad_k, grad_v, grad_gain_q, grad_gain_k = outs
    return (
        attended.reshape(1, 1, slots, width),
        grad_q.reshape(1, 1, tokens, width),
        grad_k.reshape(1, 1, tokens, width),
        grad_v.reshape(1, 1, tokens, width),
        grad_gain_q.reshape(piece),
        grad_gain_k.reshape(piece),
    )


def solution(mesh):
    token = P("dp", "fsdp", None, None)
    index = P("dp", "fsdp", None)
    return jax.shard_map(
        shards,
        mesh=mesh,
        in_specs=(token, token, token, P("fsdp"), P("fsdp"), index, index, index, token),
        out_specs=(token, token, token, token, P("fsdp"), P("fsdp")),
        check_vma=False,
    )
```

```python
import functools

import jax
import jax.numpy as jnp
from jax import lax
from jax.experimental import pallas as pl
from jax.experimental.pallas import tpu as pltpu
from jax.sharding import PartitionSpec as P

HDIM = 128
TILE = 16
PER = 3
EPS = 1e-06
MASKED = -1e30
F32 = jnp.float32
BF16 = jnp.bfloat16
MESH = pl.DeviceIdType.MESH


def dot(a, b, dims=((1,), (0,))):
    return lax.dot_general(a, b, (dims, ((), ())), preferred_element_type=F32)


def iota(shape, dim):
    return lax.broadcasted_iota(jnp.int32, shape, dim)


def as_column(row):
    n = row.shape[1]
    same = iota((n, n), 0) == iota((n, n), 1)
    return jnp.sum(jnp.where(same, row, 0), axis=1, keepdims=True)


def head_lanes(head):
    start = head * HDIM
    if not isinstance(head, int):
        start = pl.multiple_of(start, HDIM)
    return pl.ds(start, HDIM)


def kernel(
    n_dp, n_fsdp, cap, heads, piece,
    q_hbm, k_hbm, v_hbm, do_hbm, gq_ref, gk_ref, dest_ref, slot_ref, seg_ref,
    att_out, grad_q_out, grad_k_out, grad_v_out, ggq_ref, ggk_ref,
    q_in, k_in, v_in, do_in,
    att_ref, grad_q_ref, grad_k_ref, grad_v_ref,
    pick, pick_last, unpick, pack_r, unpack_r, last_r, bias, inv_q, inv_k, inv_rq, inv_rk,
    fwd_send, fwd_recv, ret_send, ret_recv,
    gtmp, gsend, grecv, gain_q, gain_k,
    part, rs_recv, ar_send, ar_recv,
    dqn, dkn, acc_q, acc_k,
    load_sem, store_sem, fs_sem, fr_sem, bs_sem, br_sem, gs_sem, gr_sem,
):
    tokens = q_in.shape[0]
    width = q_in.shape[1]
    slots = n_dp * cap
    full = heads // PER
    left = heads % PER
    halves = n_dp // TILE
    hrow = TILE * cap
    scaling = 1.0 / HDIM**0.5
    me_d = lax.axis_index("dp")
    me_f = lax.axis_index("fsdp")

    loads = [
        pltpu.make_async_copy(src, dst, load_sem.at[i])
        for i, (src, dst) in enumerate(
            ((q_hbm, q_in), (k_hbm, k_in), (v_hbm, v_in), (do_hbm, do_in))
        )
    ]
    for load in loads:
        load.start()

    barrier = pltpu.get_barrier_semaphore()

    def greet_dp(s, carry):
        pl.semaphore_signal(
            barrier, inc=1, device_id={"dp": lax.rem(me_d + s, n_dp)}, device_id_type=MESH
        )
        return carry

    def greet_fsdp(s, carry):
        pl.semaphore_signal(
            barrier, inc=1, device_id={"fsdp": lax.rem(me_f + s, n_fsdp)}, device_id_type=MESH
        )
        return carry

    lax.fori_loop(1, n_fsdp, greet_fsdp, 0)
    lax.fori_loop(1, n_dp, greet_dp, 0)

    offset = me_f * piece
    lane0 = lax.rem(offset, HDIM)
    gtmp[...] = jnp.zeros_like(gtmp)
    gtmp[0:1, 0:piece] = gq_ref[...]
    gtmp[1:2, 0:piece] = gk_ref[...]
    placed = pltpu.roll(gtmp[...], lane0, 1)
    gsend[0:2, :] = placed[0:2, :HDIM]
    gsend[2:4, :] = placed[0:2, HDIM:]
    grecv[me_f] = gsend[...]

    route = dest_ref[...] * TILE + slot_ref[...]
    rows = iota((n_dp * TILE, tokens), 0)
    route_col = as_column(route)
    cols = iota((tokens, n_dp * TILE), 1)
    for j in range(PER):
        lanes = slice(j * tokens, (j + 1) * tokens)
        pick[:, lanes] = jnp.where(rows == route + j * cap, 1.0, 0.0).astype(BF16)
        unpick[lanes, :] = jnp.where(cols == route_col + j * cap, 1.0, 0.0).astype(BF16)
    pick_last[...] = jnp.where(rows == dest_ref[...] * TILE + (TILE - 1), 1.0, 0.0).astype(BF16)

    def inverse(src, dst):
        total = jnp.zeros((tokens, HDIM), F32)
        for h in range(heads):
            x = src[:, head_lanes(h)].astype(F32)
            total = total + x * x
        mean = jnp.sum(total, axis=1, keepdims=True) * (1.0 / width)
        dst[...] = jnp.broadcast_to(lax.rsqrt(mean + EPS), (tokens, HDIM))

    loads[0].wait()
    inverse(q_in, inv_q)
    loads[1].wait()
    inverse(k_in, inv_k)

    def thirds(value):
        high = value.astype(BF16)
        rest = value - high.astype(F32)
        middle = rest.astype(BF16)
        low = (rest - middle.astype(F32)).astype(BF16)
        return high, middle, low

    slot_col = as_column(slot_ref[...])
    lane = iota((tokens, HDIM), 1)
    extra = jnp.zeros((tokens, HDIM), F32)
    for t, inv in enumerate((inv_q, inv_k)):
        for p, third in enumerate(thirds(inv[...])):
            extra = jnp.where(lane == (2 * p + t) * cap + slot_col, third.astype(F32), extra)
    extra = extra.astype(BF16)

    def send_tiles(src, dst, first, count, send_sem, recv_sem):
        def one(s, carry):
            peer = lax.rem(me_d + s, n_dp)
            pltpu.make_async_remote_copy(
                src_ref=src.at[peer, pl.ds(first, count)],
                dst_ref=dst.at[me_d, pl.ds(first, count)],
                send_sem=send_sem,
                recv_sem=recv_sem,
                device_id={"dp": peer},
                device_id_type=MESH,
            ).start()
            return carry

        lax.fori_loop(1, n_dp, one, 0)
        dst[me_d, pl.ds(first, count)] = src[me_d, pl.ds(first, count)]

    def wait_tiles(buf, first, count, sem):
        ref = buf.at[pl.ds(0, n_dp - 1), pl.ds(first, count)]
        pltpu.make_async_copy(ref, ref, sem).wait()

    def pack(blocks, tile, last=None):
        out = dot(pick[...], jnp.concatenate(blocks, axis=0))
        if last is not None:
            out = out + dot(pick_last[...], last)
        fwd_send[:, tile] = out.astype(BF16).reshape(n_dp, TILE, HDIM)

    def q_block(h):
        return q_in[:, head_lanes(h)]

    def k_block(h):
        return k_in[:, head_lanes(h)]

    def v_block(h):
        return v_in[:, head_lanes(h)]

    def pack_group(g, last=None):
        h = g * PER
        pack([q_block(h), k_block(h), q_block(h + 1)], 3 * g, last)
        pack([k_block(h + 1), q_block(h + 2), k_block(h + 2)], 3 * g + 1)
        pack([v_block(h), v_block(h + 1), v_block(h + 2)], 3 * g + 2)

    loads[2].wait()
    pack_group(0, extra)

    pl.semaphore_wait(barrier, n_dp + n_fsdp - 2)

    def send_gain(s, carry):
        peer = lax.rem(me_f + s, n_fsdp)
        pltpu.make_async_remote_copy(
            src_ref=gsend,
            dst_ref=grecv.at[me_f],
            send_sem=gs_sem.at[0],
            recv_sem=gr_sem.at[0],
            device_id={"fsdp": peer},
            device_id_type=MESH,
        ).start()
        return carry

    def wait_small(buf, sem, n):
        ref = buf.at[pl.ds(0, n - 1)]
        pltpu.make_async_copy(ref, ref, sem).wait()

    lax.fori_loop(1, n_fsdp, send_gain, 0)
    send_tiles(fwd_send, fwd_recv, 0, 3, fs_sem.at[0], fr_sem.at[0])

    def forward(g, carry):
        pack_group(g)
        send_tiles(fwd_send, fwd_recv, 3 * g, 3, fs_sem.at[g], fr_sem.at[g])
        return carry

    lax.fori_loop(1, full, forward, 0)
    for i in range(left):
        h = full * PER + i
        pack([q_block(h), k_block(h), v_block(h)], 3 * full + i)
    if left:
        send_tiles(fwd_send, fwd_recv, 3 * full, left, fs_sem.at[full], fr_sem.at[full])

    big = iota((PER * hrow, TILE * TILE), 0)
    small = iota((PER * hrow, TILE * TILE), 1)
    block, inner_row = big // hrow, big % hrow
    want = (inner_row // cap) * TILE + block * cap + inner_row % cap
    unpack_r[...] = jnp.where(want == small, 1.0, 0.0).astype(BF16)
    small = iota((TILE * TILE, PER * hrow), 0)
    big = iota((TILE * TILE, PER * hrow), 1)
    block, inner_row = big // hrow, big % hrow
    want = (inner_row // cap) * TILE + block * cap + inner_row % cap
    pack_r[...] = jnp.where(want == small, 1.0, 0.0).astype(BF16)
    small = iota((hrow, TILE * TILE), 1)
    want = (iota((hrow, TILE * TILE), 0) // cap) * TILE + (TILE - 1)
    last_r[...] = jnp.where(want == small, 1.0, 0.0).astype(BF16)
    seg_row = seg_ref[...]
    seg_col = as_column(seg_row)
    bias[...] = jnp.where((seg_col == seg_row) & (seg_col >= 0), 0.0, MASKED)

    wait_small(grecv, gr_sem.at[0], n_fsdp)
    for h in range(heads):
        for which, dst in ((0, gain_q), (1, gain_k)):
            total = jnp.zeros((1, HDIM), F32)
            for i in range(n_fsdp):
                first = i * piece // HDIM
                last = (i * piece + piece - 1) // HDIM
                if first == h:
                    total = total + grecv[i, which : which + 1, :]
                elif last == h:
                    total = total + grecv[i, which + 2 : which + 3, :]
            dst[h : h + 1, :] = total

    def unpack(buf, tile):
        out = []
        for a in range(halves):
            x = buf[a * TILE : (a + 1) * TILE, tile].reshape(TILE * TILE, HDIM)
            out.append(dot(unpack_r[...], x))
        return [
            jnp.concatenate([o[j * hrow : (j + 1) * hrow] for o in out], axis=0)
            for j in range(PER)
        ]

    def read_inverses():
        out = []
        for a in range(halves):
            x = fwd_recv[a * TILE : (a + 1) * TILE, 0].reshape(TILE * TILE, HDIM)
            out.append(dot(last_r[...], x))
        both = jnp.concatenate(out, axis=0)
        lane = iota((slots, HDIM), 1)
        at = iota((slots, HDIM), 0) % cap
        for t, dst in enumerate((inv_rq, inv_rk)):
            total = jnp.zeros((slots, HDIM), F32)
            for p in range(3):
                one = jnp.where(lane == (2 * p + t) * cap + at, both, 0.0)
                total = total + jnp.sum(one, axis=1, keepdims=True)
            dst[...] = total

    def pack_back(blocks, tile):
        for a in range(halves):
            x = jnp.concatenate([b[a * hrow : (a + 1) * hrow] for b in blocks], axis=0)
            out = dot(pack_r[...], x).astype(BF16)
            ret_send[a * TILE : (a + 1) * TILE, tile] = out.reshape(TILE, TILE, HDIM)

    valid = jnp.where(seg_row >= 0, 1.0, 0.0)

    def attend(h, q, k, v):
        do = do_in[:, head_lanes(h)]
        q = (q * inv_rq[...] * gain_q[pl.ds(h, 1), :]).astype(BF16)
        k = (k * inv_rk[...] * gain_k[pl.ds(h, 1), :]).astype(BF16)
        v = v.astype(BF16)
        st = dot(k, q, ((1,), (1,))) * scaling + bias[...]
        w = jnp.exp(st - jnp.max(st, axis=0, keepdims=True))
        pt = w * (valid / jnp.sum(w, axis=0, keepdims=True))
        ptb = pt.astype(BF16)
        att_ref[:, head_lanes(h)] = dot(ptb, v, ((0,), (0,))).astype(BF16)
        dpt = dot(v, do, ((1,), (1,)))
        inner = jnp.sum(dpt * pt, axis=0, keepdims=True)
        dst = (pt * (dpt - inner) * scaling).astype(BF16)
        dv = dot(ptb, do).astype(BF16)
        dk = dot(dst, q)
        dq = dot(dst, k, ((0,), (0,)))
        sum_q = jnp.sum(dq * q.astype(F32), axis=0, keepdims=True)
        sum_k = jnp.sum(dk * k.astype(F32), axis=0, keepdims=True)
        part[h + 1, 0:1, :] = sum_q
        part[h + 1, 1:2, :] = sum_k
        part[h, 2:3, :] = sum_q
        part[h, 3:4, :] = sum_k
        return dq.astype(BF16), dk.astype(BF16), dv

    part[...] = jnp.zeros_like(part)
    loads[3].wait()
    wait_tiles(fwd_recv, 0, 3, fr_sem.at[0])
    read_inverses()

    def group(g):
        h = g * PER
        q0, k0, q1 = unpack(fwd_recv, 3 * g)
        k1, q2, k2 = unpack(fwd_recv, 3 * g + 1)
        v0, v1, v2 = unpack(fwd_recv, 3 * g + 2)
        dq0, dk0, dv0 = attend(h, q0, k0, v0)
        dq1, dk1, dv1 = attend(h + 1, q1, k1, v1)
        dq2, dk2, dv2 = attend(h + 2, q2, k2, v2)
        pack_back([dq0, dk0, dq1], 3 * g)
        pack_back([dk1, dq2, dk2], 3 * g + 1)
        pack_back([dv0, dv1, dv2], 3 * g + 2)

    def group_step(g, carry):
        wait_tiles(fwd_recv, 3 * g, 3, fr_sem.at[g])
        group(g)
        return carry

    def back(g, carry):
        send_tiles(ret_send, ret_recv, 3 * g, 3, bs_sem.at[g], br_sem.at[g])
        return carry

    final = full - 1
    group(0)
    lax.fori_loop(1, final, group_step, 0)
    wait_tiles(fwd_recv, 3 * final, 3, fr_sem.at[final])
    if left:
        wait_tiles(fwd_recv, 3 * full, left, fr_sem.at[full])
    lax.fori_loop(0, final, back, 0)
    group(final)
    back(final, 0)
    for i in range(left):
        q, k, v = unpack(fwd_recv, 3 * full + i)
        pack_back(attend(full * PER + i, q, k, v), 3 * full + i)

    stores = [
        pltpu.make_async_copy(src, dst, store_sem.at[i])
        for i, (src, dst) in enumerate(
            (
                (att_ref, att_out),
                (grad_v_ref, grad_v_out),
                (grad_q_ref, grad_q_out),
                (grad_k_ref, grad_k_out),
            )
        )
    ]
    stores[0].start()

    def scatter(s, carry):
        peer = lax.rem(me_f + s, n_fsdp)
        pltpu.make_async_remote_copy(
            src_ref=part.at[(peer * piece) // HDIM + 1],
            dst_ref=rs_recv.at[me_f],
            send_sem=gs_sem.at[1],
            recv_sem=gr_sem.at[1],
            device_id={"fsdp": peer},
            device_id_type=MESH,
        ).start()
        return carry

    lax.fori_loop(1, n_fsdp, scatter, 0)
    rs_recv[me_f] = part[offset // HDIM + 1]
    if left:
        send_tiles(ret_send, ret_recv, 3 * full, left, bs_sem.at[full], br_sem.at[full])

    def unpack_home(tile):
        x = ret_recv[:, tile].reshape(n_dp * TILE, HDIM)
        out = dot(unpick[...], x)
        return [out[j * tokens : (j + 1) * tokens] for j in range(PER)]

    def keep(h, grad, raw, inv, gain, dst, acc):
        unit = raw[:, head_lanes(h)].astype(F32) * inv[...]
        acc[...] += grad * gain[pl.ds(h, 1), :] * unit
        dst[:, head_lanes(h)] = grad.astype(BF16)

    def keep_q(h, grad):
        keep(h, grad, q_in, inv_q, gain_q, dqn, acc_q)

    def keep_k(h, grad):
        keep(h, grad, k_in, inv_k, gain_k, dkn, acc_k)

    acc_q[...] = jnp.zeros_like(acc_q)
    acc_k[...] = jnp.zeros_like(acc_k)

    def home(g):
        h = g * PER
        wait_tiles(ret_recv, 3 * g, 3, br_sem.at[g])
        dq0, dk0, dq1 = unpack_home(3 * g)
        keep_q(h, dq0)
        keep_k(h, dk0)
        keep_q(h + 1, dq1)
        dk1, dq2, dk2 = unpack_home(3 * g + 1)
        keep_k(h + 1, dk1)
        keep_q(h + 2, dq2)
        keep_k(h + 2, dk2)
        for j, dv in enumerate(unpack_home(3 * g + 2)):
            grad_v_ref[:, head_lanes(h + j)] = dv.astype(BF16)

    def home_step(g, carry):
        home(g)
        return carry

    wait_small(rs_recv, gr_sem.at[1], n_fsdp)
    ar_send[...] = jnp.sum(rs_recv[...], axis=0)

    def share(s, carry):
        pltpu.make_async_remote_copy(
            src_ref=ar_send,
            dst_ref=ar_recv.at[me_d],
            send_sem=gs_sem.at[2],
            recv_sem=gr_sem.at[2],
            device_id={"dp": lax.rem(me_d + s, n_dp)},
            device_id_type=MESH,
        ).start()
        return carry

    lax.fori_loop(1, n_dp, share, 0)
    ar_recv[me_d] = ar_send[...]

    lax.fori_loop(0, full, home_step, 0)

    if left:
        wait_tiles(ret_recv, 3 * full, left, br_sem.at[full])
        for i in range(left):
            h = full * PER + i
            dq, dk, dv = unpack_home(3 * full + i)
            keep_q(h, dq)
            keep_k(h, dk)
            grad_v_ref[:, head_lanes(h)] = dv.astype(BF16)

    stores[1].start()
    for raw, inv, gain, src, acc, dst, store in (
        (q_in, inv_q, gain_q, dqn, acc_q, grad_q_ref, stores[2]),
        (k_in, inv_k, gain_k, dkn, acc_k, grad_k_ref, stores[3]),
    ):
        mean = jnp.sum(acc[...], axis=1, keepdims=True) * (1.0 / width)
        factor = inv[...]
        for h in range(heads):
            lanes = head_lanes(h)
            unit = raw[:, lanes].astype(F32) * factor
            grad = src[:, lanes].astype(F32) * gain[h : h + 1, :]
            dst[:, lanes] = (factor * (grad - unit * mean)).astype(BF16)
        store.start()

    wait_small(ar_recv, gr_sem.at[2], n_dp)
    total = jnp.sum(ar_recv[...], axis=0)
    gtmp[0:2, :HDIM] = total[0:2, :]
    gtmp[0:2, HDIM:] = total[2:4, :]
    mine = pltpu.roll(gtmp[...], lax.rem(2 * HDIM - lane0, 2 * HDIM), 1)
    ggq_ref[...] = mine[0:1, 0:piece] / gq_ref[...]
    ggk_ref[...] = mine[1:2, 0:piece] / gk_ref[...]

    for g in range(full):
        wait_tiles(fwd_send, 3 * g, 3, fs_sem.at[g])
        wait_tiles(ret_send, 3 * g, 3, bs_sem.at[g])
    if left:
        wait_tiles(fwd_send, 3 * full, left, fs_sem.at[full])
        wait_tiles(ret_send, 3 * full, left, bs_sem.at[full])
    for store in stores:
        store.wait()
    wait_small(grecv, gs_sem.at[0], n_fsdp)
    wait_small(rs_recv, gs_sem.at[1], n_fsdp)
    wait_small(ar_recv, gs_sem.at[2], n_dp)


def store_kernel(*refs):
    sources, targets, held = refs[:6], refs[6:12], refs[12:18]
    load_sem, store_sem = refs[18:]
    loads = [pltpu.make_async_copy(sources[i], held[i], load_sem.at[i]) for i in range(6)]
    stores = [pltpu.make_async_copy(held[i], targets[i], store_sem.at[i]) for i in range(6)]
    for load in loads:
        load.start()
    for load, store in zip(loads, stores):
        load.wait()
        store.start()
    for store in stores:
        store.wait()


def shards(q_raw, k_raw, v_raw, gain_q, gain_k, dest, slot, recv_image, d_attended):
    tokens, width = q_raw.shape[2:]
    n_dp, n_fsdp = lax.axis_size("dp"), lax.axis_size("fsdp")
    slots = recv_image.shape[2]
    cap = slots // n_dp
    heads = width // HDIM
    piece = gain_q.shape[0]
    full, left = heads // PER, heads % PER
    tiles = 3 * full + left
    vmem = pl.BlockSpec(memory_space=pltpu.VMEM)
    hbm = pl.BlockSpec(memory_space=pltpu.HBM)
    rows = pltpu.VMEM((tokens, width), BF16)
    moved = pltpu.VMEM((n_dp, tiles, TILE, HDIM), BF16)
    square = pltpu.VMEM((tokens, HDIM), F32)
    sem = pltpu.SemaphoreType.DMA
    hrow = TILE * cap
    grid_rows = (heads + 15) // 8 * 8
    outs = pl.pallas_call(
        functools.partial(kernel, n_dp, n_fsdp, cap, heads, piece),
        out_shape=(
            jax.ShapeDtypeStruct((slots, width), BF16),
            jax.ShapeDtypeStruct((tokens, width), BF16),
            jax.ShapeDtypeStruct((tokens, width), BF16),
            jax.ShapeDtypeStruct((tokens, width), BF16),
            jax.ShapeDtypeStruct((1, piece), F32),
            jax.ShapeDtypeStruct((1, piece), F32),
        ),
        in_specs=[hbm] * 4 + [vmem] * 5,
        out_specs=[hbm] * 4 + [vmem] * 2,
        scratch_shapes=[
            rows, rows, rows, pltpu.VMEM((slots, width), BF16),
            pltpu.VMEM((slots, width), BF16), rows, rows, rows,
            pltpu.VMEM((n_dp * TILE, PER * tokens), BF16),
            pltpu.VMEM((n_dp * TILE, tokens), BF16),
            pltpu.VMEM((PER * tokens, n_dp * TILE), BF16),
            pltpu.VMEM((TILE * TILE, PER * hrow), BF16),
            pltpu.VMEM((PER * hrow, TILE * TILE), BF16),
            pltpu.VMEM((hrow, TILE * TILE), BF16),
            pltpu.VMEM((slots, slots), F32),
            square, square, pltpu.VMEM((slots, HDIM), F32), pltpu.VMEM((slots, HDIM), F32),
            moved, moved, moved, moved,
            pltpu.VMEM((8, 2 * HDIM), F32),
            pltpu.VMEM((4, HDIM), F32),
            pltpu.VMEM((n_fsdp, 4, HDIM), F32),
            pltpu.VMEM((grid_rows, HDIM), F32),
            pltpu.VMEM((grid_rows, HDIM), F32),
            pltpu.VMEM((heads + 1, 4, HDIM), F32),
            pltpu.VMEM((n_fsdp, 4, HDIM), F32),
            pltpu.VMEM((4, HDIM), F32),
            pltpu.VMEM((n_dp, 4, HDIM), F32),
            rows, rows, square, square,
            sem((4,)), sem((4,)), sem((full + 1,)), sem((full + 1,)), sem((full + 1,)), sem((full + 1,)),
            sem((3,)), sem((3,)),
        ],
        compiler_params=pltpu.CompilerParams(
            collective_id=0, has_side_effects=True, vmem_limit_bytes=56 * 1024 * 1024
        ),
        name="route_attend",
    )(
        q_raw.reshape(tokens, width),
        k_raw.reshape(tokens, width),
        v_raw.reshape(tokens, width),
        d_attended.reshape(slots, width),
        gain_q.reshape(1, piece),
        gain_k.reshape(1, piece),
        dest.reshape(1, tokens),
        slot.reshape(1, tokens),
        recv_image.reshape(1, slots),
    )
    outs = pl.pallas_call(
        store_kernel,
        out_shape=tuple(jax.ShapeDtypeStruct(o.shape, o.dtype) for o in outs),
        in_specs=[pl.BlockSpec(memory_space=pl.ANY)] * 6,
        out_specs=[pl.BlockSpec(memory_space=pl.ANY)] * 6,
        scratch_shapes=[pltpu.VMEM(o.shape, o.dtype) for o in outs] + [sem((6,)), sem((6,))],
        compiler_params=pltpu.CompilerParams(vmem_limit_bytes=56 * 1024 * 1024),
        name="store",
    )(*outs)
    attended, grad_q, grad_k, grad_v, grad_gain_q, grad_gain_k = outs
    return (
        attended.reshape(1, 1, slots, width),
        grad_q.reshape(1, 1, tokens, width),
        grad_k.reshape(1, 1, tokens, width),
        grad_v.reshape(1, 1, tokens, width),
        grad_gain_q.reshape(piece),
        grad_gain_k.reshape(piece),
    )


def solution(mesh):
    token = P("dp", "fsdp", None, None)
    index = P("dp", "fsdp", None)
    return jax.shard_map(
        shards,
        mesh=mesh,
        in_specs=(token, token, token, P("fsdp"), P("fsdp"), index, index, index, token),
        out_specs=(token, token, token, token, P("fsdp"), P("fsdp")),
        check_vma=False,
    )
```

```python
import functools

import jax
import jax.numpy as jnp
from jax import lax
from jax.experimental import pallas as pl
from jax.experimental.pallas import tpu as pltpu
from jax.sharding import PartitionSpec as P

HDIM = 128
TILE = 16
PER = 3
EPS = 1e-06
MASKED = -1e30
F32 = jnp.float32
BF16 = jnp.bfloat16
MESH = pl.DeviceIdType.MESH


def dot(a, b, dims=((1,), (0,))):
    return lax.dot_general(a, b, (dims, ((), ())), preferred_element_type=F32)


def iota(shape, dim):
    return lax.broadcasted_iota(jnp.int32, shape, dim)


def as_column(row):
    n = row.shape[1]
    same = iota((n, n), 0) == iota((n, n), 1)
    return jnp.sum(jnp.where(same, row, 0), axis=1, keepdims=True)


def head_lanes(head):
    start = head * HDIM
    if not isinstance(head, int):
        start = pl.multiple_of(start, HDIM)
    return pl.ds(start, HDIM)


def kernel(
    n_dp, n_fsdp, cap, heads, piece,
    q_hbm, k_hbm, v_hbm, do_hbm, gq_hbm, gk_hbm, dest_hbm, slot_hbm, seg_hbm,
    att_out, grad_q_out, grad_k_out, grad_v_out, ggq_ref, ggk_ref,
    q_in, k_in, v_in, do_in, gq_ref, gk_ref, dest_ref, slot_ref, seg_ref,
    att_ref, grad_q_ref, grad_k_ref, grad_v_ref,
    pick, pick_last, unpick, pack_r, unpack_r, last_r, bias, inv_q, inv_k, inv_rq, inv_rk,
    fwd_send, fwd_recv, ret_send, ret_recv,
    gtmp, gsend, grecv, gain_q, gain_k,
    part, rs_recv, ar_send, ar_recv,
    dqn, dkn, acc_q, acc_k,
    load_sem, store_sem, fs_sem, fr_sem, bs_sem, br_sem, gs_sem, gr_sem,
):
    tokens = q_in.shape[0]
    width = q_in.shape[1]
    slots = n_dp * cap
    full = heads // PER
    left = heads % PER
    halves = n_dp // TILE
    hrow = TILE * cap
    scaling = 1.0 / HDIM**0.5
    me_d = lax.axis_index("dp")
    me_f = lax.axis_index("fsdp")

    loads = [
        pltpu.make_async_copy(src, dst, load_sem.at[i])
        for i, (src, dst) in enumerate(
            (
                (q_hbm, q_in), (k_hbm, k_in), (v_hbm, v_in), (do_hbm, do_in),
                (gq_hbm, gq_ref), (gk_hbm, gk_ref),
                (dest_hbm, dest_ref), (slot_hbm, slot_ref), (seg_hbm, seg_ref),
            )
        )
    ]
    for load in loads[4:]:
        load.start()
    for load in loads[:4]:
        load.start()

    barrier = pltpu.get_barrier_semaphore()

    def greet_dp(s, carry):
        pl.semaphore_signal(
            barrier, inc=1, device_id={"dp": lax.rem(me_d + s, n_dp)}, device_id_type=MESH
        )
        return carry

    def greet_fsdp(s, carry):
        pl.semaphore_signal(
            barrier, inc=1, device_id={"fsdp": lax.rem(me_f + s, n_fsdp)}, device_id_type=MESH
        )
        return carry

    lax.fori_loop(1, n_dp, greet_dp, 0)
    lax.fori_loop(1, n_fsdp, greet_fsdp, 0)
    for load in loads[4:]:
        load.wait()

    offset = me_f * piece
    lane0 = lax.rem(offset, HDIM)
    gtmp[...] = jnp.zeros_like(gtmp)
    gtmp[0:1, 0:piece] = gq_ref[...]
    gtmp[1:2, 0:piece] = gk_ref[...]
    placed = pltpu.roll(gtmp[...], lane0, 1)
    gsend[0:2, :] = placed[0:2, :HDIM]
    gsend[2:4, :] = placed[0:2, HDIM:]
    grecv[me_f] = gsend[...]

    route = dest_ref[...] * TILE + slot_ref[...]
    rows = iota((n_dp * TILE, tokens), 0)
    route_col = as_column(route)
    cols = iota((tokens, n_dp * TILE), 1)
    for j in range(PER):
        lanes = slice(j * tokens, (j + 1) * tokens)
        pick[:, lanes] = jnp.where(rows == route + j * cap, 1.0, 0.0).astype(BF16)
        unpick[lanes, :] = jnp.where(cols == route_col + j * cap, 1.0, 0.0).astype(BF16)
    pick_last[...] = jnp.where(rows == dest_ref[...] * TILE + (TILE - 1), 1.0, 0.0).astype(BF16)

    def inverse(src, dst):
        total = jnp.zeros((tokens, HDIM), F32)
        for h in range(heads):
            x = src[:, head_lanes(h)].astype(F32)
            total = total + x * x
        mean = jnp.sum(total, axis=1, keepdims=True) * (1.0 / width)
        dst[...] = jnp.broadcast_to(lax.rsqrt(mean + EPS), (tokens, HDIM))

    loads[0].wait()
    inverse(q_in, inv_q)
    loads[1].wait()
    inverse(k_in, inv_k)

    def thirds(value):
        high = value.astype(BF16)
        rest = value - high.astype(F32)
        middle = rest.astype(BF16)
        low = (rest - middle.astype(F32)).astype(BF16)
        return high, middle, low

    slot_col = as_column(slot_ref[...])
    lane = iota((tokens, HDIM), 1)
    extra = jnp.zeros((tokens, HDIM), F32)
    for t, inv in enumerate((inv_q, inv_k)):
        for p, third in enumerate(thirds(inv[...])):
            extra = jnp.where(lane == (2 * p + t) * cap + slot_col, third.astype(F32), extra)
    extra = extra.astype(BF16)

    def send_tiles(src, dst, first, count, send_sem, recv_sem):
        def one(s, carry):
            peer = lax.rem(me_d + s, n_dp)
            pltpu.make_async_remote_copy(
                src_ref=src.at[peer, pl.ds(first, count)],
                dst_ref=dst.at[me_d, pl.ds(first, count)],
                send_sem=send_sem,
                recv_sem=recv_sem,
                device_id={"dp": peer},
                device_id_type=MESH,
            ).start()
            return carry

        lax.fori_loop(1, n_dp, one, 0)
        dst[me_d, pl.ds(first, count)] = src[me_d, pl.ds(first, count)]

    def wait_tiles(buf, first, count, sem):
        ref = buf.at[pl.ds(0, n_dp - 1), pl.ds(first, count)]
        pltpu.make_async_copy(ref, ref, sem).wait()

    def pack(blocks, tile, last=None):
        out = dot(pick[...], jnp.concatenate(blocks, axis=0))
        if last is not None:
            out = out + dot(pick_last[...], last)
        fwd_send[:, tile] = out.astype(BF16).reshape(n_dp, TILE, HDIM)

    def q_block(h):
        return q_in[:, head_lanes(h)]

    def k_block(h):
        return k_in[:, head_lanes(h)]

    def v_block(h):
        return v_in[:, head_lanes(h)]

    def pack_group(g, last=None):
        h = g * PER
        pack([q_block(h), k_block(h), q_block(h + 1)], 3 * g, last)
        pack([k_block(h + 1), q_block(h + 2), k_block(h + 2)], 3 * g + 1)
        pack([v_block(h), v_block(h + 1), v_block(h + 2)], 3 * g + 2)

    loads[2].wait()
    pack_group(0, extra)

    pl.semaphore_wait(barrier, n_dp + n_fsdp - 2)

    def send_gain(s, carry):
        peer = lax.rem(me_f + s, n_fsdp)
        pltpu.make_async_remote_copy(
            src_ref=gsend,
            dst_ref=grecv.at[me_f],
            send_sem=gs_sem.at[0],
            recv_sem=gr_sem.at[0],
            device_id={"fsdp": peer},
            device_id_type=MESH,
        ).start()
        return carry

    def wait_small(buf, sem, n):
        ref = buf.at[pl.ds(0, n - 1)]
        pltpu.make_async_copy(ref, ref, sem).wait()

    lax.fori_loop(1, n_fsdp, send_gain, 0)
    send_tiles(fwd_send, fwd_recv, 0, 3, fs_sem.at[0], fr_sem.at[0])

    def forward(g, carry):
        pack_group(g)
        send_tiles(fwd_send, fwd_recv, 3 * g, 3, fs_sem.at[g], fr_sem.at[g])
        return carry

    lax.fori_loop(1, full, forward, 0)
    for i in range(left):
        h = full * PER + i
        pack([q_block(h), k_block(h), v_block(h)], 3 * full + i)
    if left:
        send_tiles(fwd_send, fwd_recv, 3 * full, left, fs_sem.at[full], fr_sem.at[full])

    big = iota((PER * hrow, TILE * TILE), 0)
    small = iota((PER * hrow, TILE * TILE), 1)
    block, inner_row = big // hrow, big % hrow
    want = (inner_row // cap) * TILE + block * cap + inner_row % cap
    unpack_r[...] = jnp.where(want == small, 1.0, 0.0).astype(BF16)
    small = iota((TILE * TILE, PER * hrow), 0)
    big = iota((TILE * TILE, PER * hrow), 1)
    block, inner_row = big // hrow, big % hrow
    want = (inner_row // cap) * TILE + block * cap + inner_row % cap
    pack_r[...] = jnp.where(want == small, 1.0, 0.0).astype(BF16)
    small = iota((hrow, TILE * TILE), 1)
    want = (iota((hrow, TILE * TILE), 0) // cap) * TILE + (TILE - 1)
    last_r[...] = jnp.where(want == small, 1.0, 0.0).astype(BF16)
    seg_row = seg_ref[...]
    seg_col = as_column(seg_row)
    bias[...] = jnp.where((seg_col == seg_row) & (seg_col >= 0), 0.0, MASKED)

    wait_small(grecv, gr_sem.at[0], n_fsdp)
    for h in range(heads):
        for which, dst in ((0, gain_q), (1, gain_k)):
            total = jnp.zeros((1, HDIM), F32)
            for i in range(n_fsdp):
                first = i * piece // HDIM
                last = (i * piece + piece - 1) // HDIM
                if first == h:
                    total = total + grecv[i, which : which + 1, :]
                elif last == h:
                    total = total + grecv[i, which + 2 : which + 3, :]
            dst[h : h + 1, :] = total

    def unpack(buf, tile):
        out = []
        for a in range(halves):
            x = buf[a * TILE : (a + 1) * TILE, tile].reshape(TILE * TILE, HDIM)
            out.append(dot(unpack_r[...], x))
        return [
            jnp.concatenate([o[j * hrow : (j + 1) * hrow] for o in out], axis=0)
            for j in range(PER)
        ]

    def read_inverses():
        out = []
        for a in range(halves):
            x = fwd_recv[a * TILE : (a + 1) * TILE, 0].reshape(TILE * TILE, HDIM)
            out.append(dot(last_r[...], x))
        both = jnp.concatenate(out, axis=0)
        lane = iota((slots, HDIM), 1)
        at = iota((slots, HDIM), 0) % cap
        for t, dst in enumerate((inv_rq, inv_rk)):
            total = jnp.zeros((slots, HDIM), F32)
            for p in range(3):
                one = jnp.where(lane == (2 * p + t) * cap + at, both, 0.0)
                total = total + jnp.sum(one, axis=1, keepdims=True)
            dst[...] = total

    def pack_back(blocks, tile):
        for a in range(halves):
            x = jnp.concatenate([b[a * hrow : (a + 1) * hrow] for b in blocks], axis=0)
            out = dot(pack_r[...], x).astype(BF16)
            ret_send[a * TILE : (a + 1) * TILE, tile] = out.reshape(TILE, TILE, HDIM)

    valid = jnp.where(seg_row >= 0, 1.0, 0.0)

    def attend(h, q, k, v):
        do = do_in[:, head_lanes(h)]
        q = (q * inv_rq[...] * gain_q[pl.ds(h, 1), :]).astype(BF16)
        k = (k * inv_rk[...] * gain_k[pl.ds(h, 1), :]).astype(BF16)
        v = v.astype(BF16)
        st = dot(k, q, ((1,), (1,))) * scaling + bias[...]
        w = jnp.exp(st - jnp.max(st, axis=0, keepdims=True))
        pt = w * (valid / jnp.sum(w, axis=0, keepdims=True))
        ptb = pt.astype(BF16)
        att_ref[:, head_lanes(h)] = dot(ptb, v, ((0,), (0,))).astype(BF16)
        dpt = dot(v, do, ((1,), (1,)))
        inner = jnp.sum(dpt * pt, axis=0, keepdims=True)
        dst = (pt * (dpt - inner) * scaling).astype(BF16)
        dv = dot(ptb, do).astype(BF16)
        dk = dot(dst, q)
        dq = dot(dst, k, ((0,), (0,)))
        sum_q = jnp.sum(dq * q.astype(F32), axis=0, keepdims=True)
        sum_k = jnp.sum(dk * k.astype(F32), axis=0, keepdims=True)
        part[h + 1, 0:1, :] = sum_q
        part[h + 1, 1:2, :] = sum_k
        part[h, 2:3, :] = sum_q
        part[h, 3:4, :] = sum_k
        return dq.astype(BF16), dk.astype(BF16), dv

    part[...] = jnp.zeros_like(part)
    loads[3].wait()
    wait_tiles(fwd_recv, 0, 3, fr_sem.at[0])
    read_inverses()

    def group(g):
        h = g * PER
        q0, k0, q1 = unpack(fwd_recv, 3 * g)
        k1, q2, k2 = unpack(fwd_recv, 3 * g + 1)
        v0, v1, v2 = unpack(fwd_recv, 3 * g + 2)
        dq0, dk0, dv0 = attend(h, q0, k0, v0)
        dq1, dk1, dv1 = attend(h + 1, q1, k1, v1)
        dq2, dk2, dv2 = attend(h + 2, q2, k2, v2)
        pack_back([dq0, dk0, dq1], 3 * g)
        pack_back([dk1, dq2, dk2], 3 * g + 1)
        pack_back([dv0, dv1, dv2], 3 * g + 2)

    def group_step(g, carry):
        wait_tiles(fwd_recv, 3 * g, 3, fr_sem.at[g])
        group(g)
        return carry

    def back(g, carry):
        send_tiles(ret_send, ret_recv, 3 * g, 3, bs_sem.at[g], br_sem.at[g])
        return carry

    final = full - 1
    group(0)
    group_step(1, 0)

    def later(g, carry):
        wait_tiles(fwd_recv, 3 * g, 3, fr_sem.at[g])
        back(g - 2, 0)
        group(g)
        return carry

    lax.fori_loop(2, final, later, 0)
    wait_tiles(fwd_recv, 3 * final, 3, fr_sem.at[final])
    if left:
        wait_tiles(fwd_recv, 3 * full, left, fr_sem.at[full])
    lax.fori_loop(final - 2, final, back, 0)
    group(final)
    back(final, 0)
    for i in range(left):
        q, k, v = unpack(fwd_recv, 3 * full + i)
        pack_back(attend(full * PER + i, q, k, v), 3 * full + i)

    stores = [
        pltpu.make_async_copy(src, dst, store_sem.at[i])
        for i, (src, dst) in enumerate(
            (
                (att_ref, att_out),
                (grad_v_ref, grad_v_out),
                (grad_q_ref, grad_q_out),
                (grad_k_ref, grad_k_out),
            )
        )
    ]
    stores[0].start()

    def scatter(s, carry):
        peer = lax.rem(me_f + s, n_fsdp)
        pltpu.make_async_remote_copy(
            src_ref=part.at[(peer * piece) // HDIM + 1],
            dst_ref=rs_recv.at[me_f],
            send_sem=gs_sem.at[1],
            recv_sem=gr_sem.at[1],
            device_id={"fsdp": peer},
            device_id_type=MESH,
        ).start()
        return carry

    lax.fori_loop(1, n_fsdp, scatter, 0)
    rs_recv[me_f] = part[offset // HDIM + 1]
    if left:
        send_tiles(ret_send, ret_recv, 3 * full, left, bs_sem.at[full], br_sem.at[full])

    def unpack_home(tile):
        x = ret_recv[:, tile].reshape(n_dp * TILE, HDIM)
        out = dot(unpick[...], x)
        return [out[j * tokens : (j + 1) * tokens] for j in range(PER)]

    def keep(h, grad, raw, inv, gain, dst, acc):
        unit = raw[:, head_lanes(h)].astype(F32) * inv[...]
        acc[...] += grad * gain[pl.ds(h, 1), :] * unit
        dst[:, head_lanes(h)] = grad.astype(BF16)

    def keep_q(h, grad):
        keep(h, grad, q_in, inv_q, gain_q, dqn, acc_q)

    def keep_k(h, grad):
        keep(h, grad, k_in, inv_k, gain_k, dkn, acc_k)

    acc_q[...] = jnp.zeros_like(acc_q)
    acc_k[...] = jnp.zeros_like(acc_k)

    def home(g):
        h = g * PER
        wait_tiles(ret_recv, 3 * g, 3, br_sem.at[g])
        dq0, dk0, dq1 = unpack_home(3 * g)
        keep_q(h, dq0)
        keep_k(h, dk0)
        keep_q(h + 1, dq1)
        dk1, dq2, dk2 = unpack_home(3 * g + 1)
        keep_k(h + 1, dk1)
        keep_q(h + 2, dq2)
        keep_k(h + 2, dk2)
        for j, dv in enumerate(unpack_home(3 * g + 2)):
            grad_v_ref[:, head_lanes(h + j)] = dv.astype(BF16)

    def home_step(g, carry):
        home(g)
        return carry

    wait_small(rs_recv, gr_sem.at[1], n_fsdp)
    ar_send[...] = jnp.sum(rs_recv[...], axis=0)

    def share(s, carry):
        pltpu.make_async_remote_copy(
            src_ref=ar_send,
            dst_ref=ar_recv.at[me_d],
            send_sem=gs_sem.at[2],
            recv_sem=gr_sem.at[2],
            device_id={"dp": lax.rem(me_d + s, n_dp)},
            device_id_type=MESH,
        ).start()
        return carry

    lax.fori_loop(1, n_dp, share, 0)
    ar_recv[me_d] = ar_send[...]

    lax.fori_loop(0, full, home_step, 0)

    if left:
        wait_tiles(ret_recv, 3 * full, left, br_sem.at[full])
        for i in range(left):
            h = full * PER + i
            dq, dk, dv = unpack_home(3 * full + i)
            keep_q(h, dq)
            keep_k(h, dk)
            grad_v_ref[:, head_lanes(h)] = dv.astype(BF16)

    stores[1].start()
    for raw, inv, gain, src, acc, dst, store in (
        (q_in, inv_q, gain_q, dqn, acc_q, grad_q_ref, stores[2]),
        (k_in, inv_k, gain_k, dkn, acc_k, grad_k_ref, stores[3]),
    ):
        mean = jnp.sum(acc[...], axis=1, keepdims=True) * (1.0 / width)
        factor = inv[...]
        for h in range(heads):
            lanes = head_lanes(h)
            unit = raw[:, lanes].astype(F32) * factor
            grad = src[:, lanes].astype(F32) * gain[h : h + 1, :]
            dst[:, lanes] = (factor * (grad - unit * mean)).astype(BF16)
        store.start()

    wait_small(ar_recv, gr_sem.at[2], n_dp)
    total = jnp.sum(ar_recv[...], axis=0)
    gtmp[0:2, :HDIM] = total[0:2, :]
    gtmp[0:2, HDIM:] = total[2:4, :]
    mine = pltpu.roll(gtmp[...], lax.rem(2 * HDIM - lane0, 2 * HDIM), 1)
    ggq_ref[...] = mine[0:1, 0:piece] / gq_ref[...]
    ggk_ref[...] = mine[1:2, 0:piece] / gk_ref[...]

    for g in range(full):
        wait_tiles(fwd_send, 3 * g, 3, fs_sem.at[g])
        wait_tiles(ret_send, 3 * g, 3, bs_sem.at[g])
    if left:
        wait_tiles(fwd_send, 3 * full, left, fs_sem.at[full])
        wait_tiles(ret_send, 3 * full, left, bs_sem.at[full])
    for store in stores:
        store.wait()
    wait_small(grecv, gs_sem.at[0], n_fsdp)
    wait_small(rs_recv, gs_sem.at[1], n_fsdp)
    wait_small(ar_recv, gs_sem.at[2], n_dp)


def store_kernel(*refs):
    sources, targets, held = refs[:6], refs[6:12], refs[12:18]
    load_sem, store_sem = refs[18:]
    loads = [pltpu.make_async_copy(sources[i], held[i], load_sem.at[i]) for i in range(6)]
    stores = [pltpu.make_async_copy(held[i], targets[i], store_sem.at[i]) for i in range(6)]
    for load in loads:
        load.start()
    for load, store in zip(loads, stores):
        load.wait()
        store.start()
    for store in stores:
        store.wait()


def shards(q_raw, k_raw, v_raw, gain_q, gain_k, dest, slot, recv_image, d_attended):
    tokens, width = q_raw.shape[2:]
    n_dp, n_fsdp = lax.axis_size("dp"), lax.axis_size("fsdp")
    slots = recv_image.shape[2]
    cap = slots // n_dp
    heads = width // HDIM
    piece = gain_q.shape[0]
    full, left = heads // PER, heads % PER
    tiles = 3 * full + left
    vmem = pl.BlockSpec(memory_space=pltpu.VMEM)
    hbm = pl.BlockSpec(memory_space=pltpu.HBM)
    rows = pltpu.VMEM((tokens, width), BF16)
    moved = pltpu.VMEM((n_dp, tiles, TILE, HDIM), BF16)
    square = pltpu.VMEM((tokens, HDIM), F32)
    sem = pltpu.SemaphoreType.DMA
    hrow = TILE * cap
    grid_rows = (heads + 15) // 8 * 8
    outs = pl.pallas_call(
        functools.partial(kernel, n_dp, n_fsdp, cap, heads, piece),
        out_shape=(
            jax.ShapeDtypeStruct((slots, width), BF16),
            jax.ShapeDtypeStruct((tokens, width), BF16),
            jax.ShapeDtypeStruct((tokens, width), BF16),
            jax.ShapeDtypeStruct((tokens, width), BF16),
            jax.ShapeDtypeStruct((1, piece), F32),
            jax.ShapeDtypeStruct((1, piece), F32),
        ),
        in_specs=[hbm] * 9,
        out_specs=[hbm] * 4 + [vmem] * 2,
        scratch_shapes=[
            rows, rows, rows, pltpu.VMEM((slots, width), BF16),
            pltpu.VMEM((1, piece), F32), pltpu.VMEM((1, piece), F32),
            pltpu.VMEM((1, tokens), jnp.int32), pltpu.VMEM((1, tokens), jnp.int32),
            pltpu.VMEM((1, slots), jnp.int32),
            pltpu.VMEM((slots, width), BF16), rows, rows, rows,
            pltpu.VMEM((n_dp * TILE, PER * tokens), BF16),
            pltpu.VMEM((n_dp * TILE, tokens), BF16),
            pltpu.VMEM((PER * tokens, n_dp * TILE), BF16),
            pltpu.VMEM((TILE * TILE, PER * hrow), BF16),
            pltpu.VMEM((PER * hrow, TILE * TILE), BF16),
            pltpu.VMEM((hrow, TILE * TILE), BF16),
            pltpu.VMEM((slots, slots), F32),
            square, square, pltpu.VMEM((slots, HDIM), F32), pltpu.VMEM((slots, HDIM), F32),
            moved, moved, moved, moved,
            pltpu.VMEM((8, 2 * HDIM), F32),
            pltpu.VMEM((4, HDIM), F32),
            pltpu.VMEM((n_fsdp, 4, HDIM), F32),
            pltpu.VMEM((grid_rows, HDIM), F32),
            pltpu.VMEM((grid_rows, HDIM), F32),
            pltpu.VMEM((heads + 1, 4, HDIM), F32),
            pltpu.VMEM((n_fsdp, 4, HDIM), F32),
            pltpu.VMEM((4, HDIM), F32),
            pltpu.VMEM((n_dp, 4, HDIM), F32),
            rows, rows, square, square,
            sem((9,)), sem((4,)), sem((full + 1,)), sem((full + 1,)), sem((full + 1,)), sem((full + 1,)),
            sem((3,)), sem((3,)),
        ],
        compiler_params=pltpu.CompilerParams(
            collective_id=0, has_side_effects=True, vmem_limit_bytes=56 * 1024 * 1024
        ),
        name="route_attend",
    )(
        q_raw.reshape(tokens, width),
        k_raw.reshape(tokens, width),
        v_raw.reshape(tokens, width),
        d_attended.reshape(slots, width),
        gain_q.reshape(1, piece),
        gain_k.reshape(1, piece),
        dest.reshape(1, tokens),
        slot.reshape(1, tokens),
        recv_image.reshape(1, slots),
    )
    outs = pl.pallas_call(
        store_kernel,
        out_shape=tuple(jax.ShapeDtypeStruct(o.shape, o.dtype) for o in outs),
        in_specs=[pl.BlockSpec(memory_space=pl.ANY)] * 6,
        out_specs=[pl.BlockSpec(memory_space=pl.ANY)] * 6,
        scratch_shapes=[pltpu.VMEM(o.shape, o.dtype) for o in outs] + [sem((6,)), sem((6,))],
        compiler_params=pltpu.CompilerParams(vmem_limit_bytes=56 * 1024 * 1024),
        name="store",
    )(*outs)
    attended, grad_q, grad_k, grad_v, grad_gain_q, grad_gain_k = outs
    return (
        attended.reshape(1, 1, slots, width),
        grad_q.reshape(1, 1, tokens, width),
        grad_k.reshape(1, 1, tokens, width),
        grad_v.reshape(1, 1, tokens, width),
        grad_gain_q.reshape(piece),
        grad_gain_k.reshape(piece),
    )


def solution(mesh):
    token = P("dp", "fsdp", None, None)
    index = P("dp", "fsdp", None)
    return jax.shard_map(
        shards,
        mesh=mesh,
        in_specs=(token, token, token, P("fsdp"), P("fsdp"), index, index, index, token),
        out_specs=(token, token, token, token, P("fsdp"), P("fsdp")),
        check_vma=False,
    )
```
